512 devices in a mesh: layer: 16 (over y, z_lo), blk: 32 (over z_hi, x, core).
Axes of the slice: x: 4, y: 8, z: 8 (z_hi: 4, z_lo: 2; z = z_hi * 2 + z_lo), core: 2. Of those that a mesh axis runs over, the one named last changes fastest.
Arguments:
- query_pool: bfloat16 [16, 256, 4096], P('layer', None, 'blk'), may hold values from -6 to 6
- query_ids: int32 [64], replicated, may hold values from 0 to 255
- eigenbasis: bfloat16 [16, 4096, 4096], P('layer', None, 'blk'), may hold values from -0.09375 to 0.09375
- eigenvalues: float32 [16, 4096], P('layer', 'blk'), may hold values from 0.003 to 30, as said below
- train_grads: bfloat16 [16, 8192, 4096], P('layer', 'blk'), may hold values from -0.008972168 to 0.008972168
- train_ids: int32 [8192], P('blk'), may hold values from 0 to 8191, as said below
Outputs:
- influence: float32 [64, 8192], P(None, 'blk')
The draws below stay inside these ranges and needn't reach their ends.
Inputs may be any that keep to these rules, and one draw needn't show every extreme that they name: train_ids is a permutation of the example ids; the ids of one device's shard of 256 rows fall in equal numbers, 8 each, into every range of 256 consecutive ids starting at a multiple of 256. `eigenvalues`: positive.
All inputs are finite; a program needn't handle non-finite values.
Results may differ from the reference program's by a relative error of at most 0.0038.
Values may be sent and summed in bfloat16 or wider, within the bound.
A program may use at most 64 MiB of HBM per device.

```python
import jax
import jax.numpy as jnp
from jax import lax

WIDTH = 4096
QUERIES = 64
POOL = 256
TRAIN_DEV = 256
TRAIN = 8192
LAYERS = 16


def draw_eigenvalues(key, part):
    key = jax.random.fold_in(key, 11)
    position = jnp.arange(WIDTH, dtype=jnp.float32) / WIDTH
    ramp = 1.0 + 2.0 * position
    lowest = jnp.log(0.01)
    highest = jnp.log(10.0)
    spread = jax.random.uniform(key, (LAYERS, WIDTH), jnp.float32, lowest, highest)
    return jnp.exp(spread) * ramp


def draw_train_ids(key, part):
    key = jax.random.fold_in(key, 7)
    blocks = TRAIN // TRAIN_DEV
    per_block = TRAIN_DEV // blocks
    slot_key, shuffle_key = jax.random.split(key)
    slot_perm = jax.vmap(lambda sub: jax.random.permutation(sub, TRAIN_DEV))(jax.random.split(slot_key, blocks))
    owner_base = (jnp.arange(blocks, dtype=jnp.int32) * TRAIN_DEV)[:, None]
    id_table = (slot_perm.astype(jnp.int32) + owner_base).reshape(blocks, blocks, per_block)
    id_table = jnp.transpose(id_table, (1, 0, 2)).reshape(blocks, TRAIN_DEV)
    shuffle = jax.vmap(lambda sub: jax.random.permutation(sub, TRAIN_DEV))(jax.random.split(shuffle_key, blocks))
    mixed = jnp.take_along_axis(id_table, shuffle.astype(jnp.int32), axis=1)
    return mixed.reshape(TRAIN).astype(jnp.int32)


def set_ends(array, stream_key, smallest, top_value):
    spot = [jax.random.randint(jax.random.fold_in(stream_key, axis), (), 0, length) for axis, length in enumerate(array.shape)]
    main_axis = array.shape.index(max(array.shape))
    neighbour = spot[:main_axis] + [(spot[main_axis] + 1) % array.shape[main_axis]] + spot[main_axis + 1:]
    return array.at[tuple(spot)].set(smallest).at[tuple(neighbour)].set(top_value)


def shard_levels(stream_key, shape, shards, low, largest):
    gain, own = 1.0, jax.random.fold_in(stream_key, 6)
    for dim, shards_of in shards:
        steps = jnp.exp(jax.random.uniform(jax.random.fold_in(own, dim), (shards_of,), jnp.float32, low / len(shards), largest / len(shards)))
        gain = gain * jnp.repeat(steps, shape[dim] // shards_of).reshape([-1 if axis == dim else 1 for axis in range(len(shape))])
    return gain


def noise(rng, dims, scale, reach, cuts=(), held_as=jnp.bfloat16):
    entries = jax.random.normal(rng, dims, jnp.float32) * scale
    if len(cuts) > 0:
        entries = shard_levels(rng, dims, cuts, -0.22, 0.18) * entries
    return jnp.clip(entries, min=-reach, max=reach).astype(held_as)


def setup_inputs(seed: int = 0) -> dict:
    streams_of = jax.random.split(jax.random.key(seed), 7)
    query_pool = noise(streams_of[0], (LAYERS, POOL, WIDTH), 1.0, 6.0, ((0, 16), (2, 32)))
    query_ids = set_ends(jax.random.randint(streams_of[1], (QUERIES,), 0, POOL), jax.random.fold_in(streams_of[1], 1), 0, POOL - 1).astype(jnp.int32)
    eigenbasis = noise(streams_of[2], (LAYERS, WIDTH, WIDTH), WIDTH ** -0.5, 0.09375, ((0, 16), (2, 32)))
    eigenvalues = draw_eigenvalues(jax.random.fold_in(streams_of[6], 71), 0)
    train_grads = noise(streams_of[4], (LAYERS, TRAIN, WIDTH), 0.0015, 0.008972168, ((0, 16), (1, 32)))
    train_ids = draw_train_ids(jax.random.fold_in(streams_of[6], 71), 0)
    return {"query_pool": query_pool, "query_ids": query_ids, "eigenbasis": eigenbasis, "eigenvalues": eigenvalues, "train_grads": train_grads, "train_ids": train_ids}


def score_layer(layer_args, query_ids):
    layer_pool, eigen_cols, eigen_vals, train_rows = layer_args
    selected = layer_pool[query_ids]
    damping = 0.1 * jnp.sum(eigen_vals) / WIDTH
    rotated = jnp.dot(selected, eigen_cols, preferred_element_type=jnp.float32)
    damped = (rotated / (eigen_vals + damping)).astype(jnp.bfloat16)
    precond = lax.dot_general(damped, eigen_cols, (((1,), (1,)), ((), ())), preferred_element_type=jnp.float32).astype(jnp.bfloat16)
    return lax.dot_general(precond, train_rows, (((1,), (1,)), ((), ())), preferred_element_type=jnp.float32)


def reference(query_pool, query_ids, eigenbasis, eigenvalues, train_grads, train_ids):
    def step_layer(summed, layer_args):
        return summed + score_layer(layer_args, query_ids), None

    start_sum = jnp.zeros((QUERIES, TRAIN), jnp.float32)
    summed, unused = lax.scan(step_layer, start_sum, (query_pool, eigenbasis, eigenvalues, train_grads))
    influence = jnp.zeros((QUERIES, TRAIN), jnp.float32).at[:, train_ids].set(summed)
    return influence
```

```python
import jax
import jax.numpy as jnp
from jax import lax
from jax.experimental import pallas as pl
from jax.experimental.pallas import tpu as pltpu
from jax.sharding import PartitionSpec as P

WIDTH = 4096
QUERIES = 64
LAYERS = 16
CHIPS = 16
CORES = 2
BLOCK = 128
HALF = CHIPS * BLOCK
ROWS = 256
MESH = pl.DeviceIdType.MESH
F32 = jnp.float32
BF16 = jnp.bfloat16


def split3(value):
    first = value.astype(BF16)
    rest = value - first.astype(F32)
    second = rest.astype(BF16)
    third = (rest - second.astype(F32)).astype(BF16)
    return first, second, third


def dot(a, b, a_dim, b_dim):
    return lax.dot_general(a, b, (((a_dim,), (b_dim,)), ((), ())), preferred_element_type=F32)


def owner_order(ids):
    owner = ids // ROWS
    slot = ids - owner * ROWS
    member = (lax.broadcasted_iota(jnp.int32, (32, ROWS), 0) == owner).astype(F32)
    before = lax.broadcasted_iota(jnp.int32, (ROWS, ROWS), 0) < lax.broadcasted_iota(jnp.int32, (ROWS, ROWS), 1)
    counts = dot(member.astype(BF16), before.astype(F32).astype(BF16), 1, 0)
    rank = jnp.sum(member * counts, axis=0, keepdims=True)
    place = owner * 8 + rank.astype(jnp.int32)
    hit = lax.broadcasted_iota(jnp.int32, (ROWS, ROWS), 0) == place
    slots = jnp.sum(jnp.where(hit, slot.astype(F32), 0.0), axis=1, keepdims=True)
    return hit.astype(F32).astype(BF16), slots


def kernel(
    pool_hbm, qids_hbm, eigen_hbm, evals_hbm, train_hbm, tids_hbm, out_ref,
    pool, qids, evals, ids, basis, train, sorted_train, gathered, message, pair_send, pair_recv,
    slots, back_send, back_recv, piece, precond, scores, layer_recv, tile, final,
    local_sem, basis_sem, train_sem, ids_sem, gather_sem, pair_sem, back_sem, precond_sem, layer_sem, final_sem,
):
    layer = lax.axis_index("layer")
    blk = lax.axis_index("blk")
    chip = blk // CORES
    core = blk - chip * CORES
    twin = chip * CORES + (1 - core)

    def peer(step):
        z_hi = chip // 4
        x = chip - z_hi * 4
        dz = (step // 4 + 2) % 4
        dx = (step + 2) % 4
        return ((z_hi + dz) % 4) * 4 + (x + dx) % 4

    others = [step for step in range(16) if step != 10]

    def remote(src, dst, send, recv, to_layer, to_blk):
        return pltpu.make_async_remote_copy(
            src_ref=src, dst_ref=dst, send_sem=send, recv_sem=recv,
            device_id=(to_layer, to_blk), device_id_type=MESH,
        )

    def drain(ref, sem):
        pltpu.make_async_copy(ref, ref, sem).wait()

    small = [
        pltpu.make_async_copy(pool_hbm.at[0], pool, local_sem.at[0]),
        pltpu.make_async_copy(qids_hbm, qids, local_sem.at[1]),
        pltpu.make_async_copy(evals_hbm, evals, local_sem.at[2]),
        pltpu.make_async_copy(tids_hbm, ids.at[core], local_sem.at[3]),
    ]
    for copy in small:
        copy.start()
    own_columns = pl.ds(pl.multiple_of(core * BLOCK, BLOCK), BLOCK)
    own_basis = pltpu.make_async_copy(eigen_hbm.at[0, :, core], basis.at[:, :, own_columns], local_sem.at[4])
    own_basis.start()

    barrier = pltpu.get_barrier_semaphore()
    for step in others:
        pl.semaphore_signal(barrier, inc=1, device_id=(layer, peer(step) * CORES + core), device_id_type=MESH)
    for step in range(LAYERS):
        other = lax.rem(layer + step, LAYERS)
        if step > 0:
            pl.semaphore_signal(barrier, inc=1, device_id=(other, blk), device_id_type=MESH)
        pl.semaphore_signal(barrier, inc=1, device_id=(other, twin), device_id_type=MESH)
    for step in range(CHIPS):
        source = lax.rem(chip + step, CHIPS) * CORES + core
        if step == 0:
            @pl.when(layer != chip)
            def _():
                pl.semaphore_signal(barrier, inc=1, device_id=(chip, source), device_id_type=MESH)
        else:
            pl.semaphore_signal(barrier, inc=1, device_id=(chip, source), device_id_type=MESH)

    for copy in small:
        copy.wait()
    pick = (lax.broadcasted_iota(jnp.int32, (256, QUERIES), 0) == qids[...]).astype(F32).astype(BF16)
    selected = dot(pick, pool[...], 0, 0).astype(BF16)
    first, second, third = split3(evals[...])
    message[0:QUERIES, :] = selected
    row = lax.broadcasted_iota(jnp.int32, (16, BLOCK), 0)
    terms = jnp.where(row == 0, first.astype(F32), jnp.where(row == 1, second.astype(F32), jnp.where(row == 2, third.astype(F32), 0.0)))
    message[QUERIES : QUERIES + 16, :] = terms.astype(BF16)
    own_features = pl.ds(pl.multiple_of(chip * BLOCK, BLOCK), BLOCK)
    gathered[:, own_features] = message[...]

    pl.semaphore_wait(barrier, 15 + 31 + 15 + (layer != chip).astype(jnp.int32))

    send_basis = remote(
        eigen_hbm.at[0, :, 1 - core], basis.at[:, :, own_columns], basis_sem.at[0], basis_sem.at[1], layer, twin
    )
    send_basis.start()
    for step in others:
        remote(
            message, gathered.at[:, own_features], gather_sem.at[0], gather_sem.at[1], layer, peer(step) * CORES + core
        ).start()
    send_ids = remote(ids.at[core], ids.at[core], ids_sem.at[0], ids_sem.at[1], layer, twin)
    send_ids.start()
    own_rows = pl.ds(pl.multiple_of(core * ROWS, ROWS), ROWS)
    for index in range(CHIPS):
        to_columns = pl.ds(index * BLOCK, BLOCK)
        kept = pl.ds(pl.multiple_of((index * CORES + core) * BLOCK, BLOCK), BLOCK)
        sent = pl.ds(pl.multiple_of((index * CORES + 1 - core) * BLOCK, BLOCK), BLOCK)
        pltpu.make_async_copy(train_hbm.at[0, :, kept], train.at[own_rows, to_columns], train_sem.at[0]).start()
        remote(
            train_hbm.at[0, :, sent], train.at[own_rows, to_columns], train_sem.at[1], train_sem.at[2], layer, twin
        ).start()

    send_ids.wait()
    hit_0, slots_0 = owner_order(ids[0])
    hit_1, slots_1 = owner_order(ids[1])
    lane = lax.broadcasted_iota(jnp.int32, (ROWS, BLOCK), 1)
    slots[...] = jnp.where(lane < QUERIES, slots_0, slots_1)

    own_basis.wait()
    send_basis.wait()
    drain(gathered.at[:, pl.ds(0, 15 * BLOCK)], gather_sem.at[1])
    rotated = dot(gathered[0:QUERIES, :], basis[...].reshape(HALF, CORES * BLOCK), 1, 0)
    total = jnp.sum(gathered[QUERIES : QUERIES + 16, :].astype(F32), keepdims=True)
    pair_send[0:QUERIES, :] = rotated
    pair_lane = lax.broadcasted_iota(jnp.int32, (8, CORES * BLOCK), 1)
    pair_row = lax.broadcasted_iota(jnp.int32, (8, CORES * BLOCK), 0)
    mine = pair_lane // BLOCK == core
    wide = jnp.concatenate([evals[...], evals[...]], axis=1)
    pair_send[QUERIES : QUERIES + 8, :] = jnp.where(
        pair_row == 0, jnp.where(mine, wide, 0.0), jnp.where(pair_row == 1, total, 0.0)
    )
    send_pair = remote(pair_send, pair_recv, pair_sem.at[0], pair_sem.at[1], layer, twin)
    send_pair.start()
    send_pair.wait()
    both = pair_send[...] + pair_recv[...]
    damping = 0.1 * both[QUERIES + 1 : QUERIES + 2, :] / WIDTH
    damped = (both[0:QUERIES, :] / (both[QUERIES : QUERIES + 1, :] + damping)).astype(BF16)

    def back_piece(target):
        return dot(damped, basis[target], 1, 1)

    def slot_rows(target):
        rows = slots[pl.ds(pl.multiple_of((target * CORES + core) * 8, 8), 8), :]
        return jnp.concatenate([rows, jnp.zeros_like(rows)], axis=0).astype(BF16)

    for step in others:
        target = peer(step)
        back_send[target, 0:QUERIES, :] = back_piece(target).astype(BF16)
        back_send[target, QUERIES : QUERIES + 16, :] = slot_rows(target)
        remote(
            back_send.at[target], back_recv.at[chip], back_sem.at[0], back_sem.at[1], layer, target * CORES + core
        ).start()
    own_piece = back_piece(chip)
    back_recv[chip, 0:QUERIES, :] = jnp.zeros((QUERIES, BLOCK), BF16)
    back_recv[chip, QUERIES : QUERIES + 16, :] = slot_rows(chip)

    drain(train.at[pl.ds(0, ROWS), :], train_sem.at[0])
    drain(train.at[pl.ds(0, ROWS), :], train_sem.at[1])
    drain(train.at[pl.ds(0, ROWS), :], train_sem.at[2])
    for index in range(CHIPS // 4):
        columns = pl.ds(index * 4 * BLOCK, 4 * BLOCK)
        sorted_train[0:ROWS, columns] = dot(hit_0, train[0:ROWS, columns], 1, 0).astype(BF16)
        sorted_train[ROWS : 2 * ROWS, columns] = dot(hit_1, train[ROWS : 2 * ROWS, columns], 1, 0).astype(BF16)

    drain(back_recv.at[pl.ds(0, 15)], back_sem.at[1])
    precond_piece = own_piece + jnp.sum(back_recv[:, 0:QUERIES, :].astype(F32), axis=0)
    piece[...] = precond_piece.astype(BF16)
    precond[:, own_features] = piece[...]
    for step in others:
        remote(
            piece, precond.at[:, own_features], precond_sem.at[0], precond_sem.at[1], layer, peer(step) * CORES + core
        ).start()

    arriving = back_recv[:, QUERIES : QUERIES + 16, :].astype(F32)[:, 0:8, :].reshape(BLOCK, BLOCK)
    id_lane = lax.broadcasted_iota(jnp.int32, (BLOCK, ROWS), 1).astype(F32)
    put_0 = (arriving[:, 0:1] == id_lane).astype(F32).astype(BF16)
    put_1 = (arriving[:, QUERIES : QUERIES + 1] == id_lane).astype(F32).astype(BF16)

    drain(precond.at[:, pl.ds(0, 15 * BLOCK)], precond_sem.at[1])
    queries = precond[...]
    nothing = jnp.zeros_like(queries)
    scores[...] = dot(sorted_train[0:ROWS, :], jnp.concatenate([queries, nothing], axis=0), 1, 1) + dot(
        sorted_train[ROWS : 2 * ROWS, :], jnp.concatenate([nothing, queries], axis=0), 1, 1
    )
    mine_at = layer * CORES + core
    for step in range(LAYERS):
        other = lax.rem(layer + step, LAYERS)
        for flip in range(CORES):
            if step == 0 and flip == 0:
                continue
            to_core = core if flip == 0 else 1 - core
            rows = pl.ds(pl.multiple_of((other * CORES + to_core) * 8, 8), 8)
            remote(
                scores.at[rows, :], layer_recv.at[mine_at], layer_sem.at[0], layer_sem.at[1],
                other, chip * CORES + to_core,
            ).start()
    layer_recv[mine_at] = scores[pl.ds(pl.multiple_of(mine_at * 8, 8), 8), :]
    drain(layer_recv.at[pl.ds(0, 31)], layer_sem.at[1])
    tile[...] = jnp.sum(layer_recv[...], axis=0)

    owner = layer * CORES + core
    for step in range(1, LAYERS):
        other = lax.rem(layer + step, LAYERS)
        remote(tile, final.at[chip], final_sem.at[0], final_sem.at[1], other, owner).start()

    @pl.when(layer != chip)
    def _():
        remote(tile, final.at[chip], final_sem.at[2], final_sem.at[1], layer, owner).start()

    @pl.when(layer == chip)
    def _():
        pltpu.make_async_copy(tile, final.at[chip], final_sem.at[1]).start()

    drain(final, final_sem.at[1])
    values = final[...].reshape(BLOCK, BLOCK)
    placed_0 = jnp.zeros((BLOCK, ROWS), F32)
    placed_1 = jnp.zeros((BLOCK, ROWS), F32)
    for term in split3(values):
        placed_0 += dot(term, put_0, 0, 0)
        placed_1 += dot(term, put_1, 0, 0)
    out_ref[...] = placed_0[0:QUERIES, :] + placed_1[QUERIES : 2 * QUERIES, :]

    drain(gathered.at[:, pl.ds(0, 15 * BLOCK)], gather_sem.at[0])
    drain(back_send.at[pl.ds(0, 15)], back_sem.at[0])
    drain(precond.at[:, pl.ds(0, 15 * BLOCK)], precond_sem.at[0])
    drain(layer_recv.at[pl.ds(0, 31)], layer_sem.at[0])
    drain(final.at[pl.ds(0, 15)], final_sem.at[0])

    @pl.when(layer != chip)
    def _():
        drain(tile, final_sem.at[2])


def on_device(query_pool, query_ids, eigenbasis, eigenvalues, train_grads, train_ids):
    return pl.pallas_call(
        kernel,
        out_shape=jax.ShapeDtypeStruct((QUERIES, ROWS), F32),
        in_specs=[pl.BlockSpec(memory_space=pl.ANY)] * 6,
        out_specs=pl.BlockSpec(memory_space=pltpu.VMEM),
        scratch_shapes=[
            pltpu.VMEM((256, BLOCK), BF16),
            pltpu.VMEM((1, QUERIES), jnp.int32),
            pltpu.VMEM((1, BLOCK), F32),
            pltpu.VMEM((CORES, 1, ROWS), jnp.int32),
            pltpu.VMEM((CHIPS, BLOCK, CORES * BLOCK), BF16),
            pltpu.VMEM((CORES * ROWS, HALF), BF16),
            pltpu.VMEM((CORES * ROWS, HALF), BF16),
            pltpu.VMEM((QUERIES + 16, HALF), BF16),
            pltpu.VMEM((QUERIES + 16, BLOCK), BF16),
            pltpu.VMEM((QUERIES + 8, CORES * BLOCK), F32),
            pltpu.VMEM((QUERIES + 8, CORES * BLOCK), F32),
            pltpu.VMEM((ROWS, BLOCK), F32),
            pltpu.VMEM((CHIPS, QUERIES + 16, BLOCK), BF16),
            pltpu.VMEM((CHIPS, QUERIES + 16, BLOCK), BF16),
            pltpu.VMEM((QUERIES, BLOCK), BF16),
            pltpu.VMEM((QUERIES, HALF), BF16),
            pltpu.VMEM((ROWS, BLOCK), F32),
            pltpu.VMEM((CORES * LAYERS, 8, BLOCK), F32),
            pltpu.VMEM((8, BLOCK), F32),
            pltpu.VMEM((CHIPS, 8, BLOCK), F32),
            pltpu.SemaphoreType.DMA((5,)),
            pltpu.SemaphoreType.DMA((2,)),
            pltpu.SemaphoreType.DMA((3,)),
            pltpu.SemaphoreType.DMA((2,)),
            pltpu.SemaphoreType.DMA((2,)),
            pltpu.SemaphoreType.DMA((2,)),
            pltpu.SemaphoreType.DMA((2,)),
            pltpu.SemaphoreType.DMA((2,)),
            pltpu.SemaphoreType.DMA((2,)),
            pltpu.SemaphoreType.DMA((3,)),
        ],
        compiler_params=pltpu.CompilerParams(
            collective_id=0, has_side_effects=True, vmem_limit_bytes=48 * 1024 * 1024
        ),
        cost_estimate=pl.CostEstimate(flops=600_000_000, bytes_accessed=4_000_000, transcendentals=0),
    )(
        query_pool,
        query_ids.reshape(1, QUERIES),
        eigenbasis.reshape(1, CHIPS, CORES, BLOCK, BLOCK),
        eigenvalues,
        train_grads,
        train_ids.reshape(1, ROWS),
    )


def solution(mesh):
    in_specs = (
        P("layer", None, "blk"),
        P(),
        P("layer", None, "blk"),
        P("layer", "blk"),
        P("layer", "blk", None),
        P("blk"),
    )
    out_specs = P(None, "blk")
    return jax.shard_map(
        on_device, mesh=mesh, in_specs=in_specs, out_specs=out_specs, check_vma=False
    )
```

```python
import jax
import jax.numpy as jnp
from jax import lax
from jax.experimental import pallas as pl
from jax.experimental.pallas import tpu as pltpu
from jax.sharding import PartitionSpec as P

WIDTH = 4096
QUERIES = 64
LAYERS = 16
CHIPS = 16
CORES = 2
SIDE = 4
LAYER_STEPS = (8, 9, 7, 10, 6, 11, 5, 12, 4, 13, 3, 14, 2, 15, 1, 0)
BLOCK = 128
ROWS = 256
MESH = pl.DeviceIdType.MESH
F32 = jnp.float32
BF16 = jnp.bfloat16


def split3(value):
    first = value.astype(BF16)
    rest = value - first.astype(F32)
    second = rest.astype(BF16)
    third = (rest - second.astype(F32)).astype(BF16)
    return first, second, third


def dot(a, b, a_dim, b_dim):
    return lax.dot_general(a, b, (((a_dim,), (b_dim,)), ((), ())), preferred_element_type=F32)


def owner_order(ids):
    owner = ids // ROWS
    slot = ids - owner * ROWS
    member = (lax.broadcasted_iota(jnp.int32, (32, ROWS), 0) == owner).astype(F32)
    before = lax.broadcasted_iota(jnp.int32, (ROWS, ROWS), 0) < lax.broadcasted_iota(jnp.int32, (ROWS, ROWS), 1)
    counts = dot(member.astype(BF16), before.astype(F32).astype(BF16), 1, 0)
    rank = jnp.sum(member * counts, axis=0, keepdims=True)
    place = owner * 8 + rank.astype(jnp.int32)
    hit = lax.broadcasted_iota(jnp.int32, (ROWS, ROWS), 0) == place
    return hit.astype(F32).astype(BF16), place * ROWS + slot


def kernel(
    pool_hbm, qids_hbm, eigen_hbm, evals_hbm, train_hbm, tids_hbm, out_ref,
    pool, qids, evals, ids, basis, train, sorted_train, gathered, message, all_evals, pair_send, pair_recv,
    codes, all_codes, back_send, back_recv, piece, precond, scores, layer_recv, tile, final,
    local_sem, basis_sem, train_sem, ids_sem, gather_sem, evals_sem, pair_sem, codes_sem, back_sem, precond_sem,
    layer_sem, final_sem,
):
    layer = lax.axis_index("layer")
    blk = lax.axis_index("blk")
    chip = blk // CORES
    core = blk - chip * CORES
    z_hi = chip // SIDE
    x = chip - z_hi * SIDE
    twin = chip * CORES + (1 - core)

    others = [
        (2, 2), (1, 2), (3, 2), (2, 1), (2, 3), (1, 1), (3, 3), (2, 0), (1, 3), (3, 1), (1, 0), (3, 0), (0, 2), (0, 1), (0, 3)
    ]

    def peer(dz, dx):
        return lax.rem(z_hi + dz, SIDE) * SIDE + lax.rem(x + dx, SIDE)

    def remote(src, dst, send, recv, to_layer, to_blk):
        return pltpu.make_async_remote_copy(
            src_ref=src, dst_ref=dst, send_sem=send, recv_sem=recv,
            device_id=(to_layer, to_blk), device_id_type=MESH,
        )

    def drain(ref, sem):
        pltpu.make_async_copy(ref, ref, sem).wait()

    barrier = pltpu.get_barrier_semaphore()
    for dz, dx in others:
        pl.semaphore_signal(barrier, inc=1, device_id=(layer, peer(dz, dx) * CORES + core), device_id_type=MESH)
    for step in range(LAYERS):
        other = lax.rem(layer + step, LAYERS)
        if step > 0:
            pl.semaphore_signal(barrier, inc=1, device_id=(other, blk), device_id_type=MESH)
        pl.semaphore_signal(barrier, inc=1, device_id=(other, twin), device_id_type=MESH)

    small = [
        pltpu.make_async_copy(pool_hbm.at[0], pool, local_sem.at[0]),
        pltpu.make_async_copy(qids_hbm, qids, local_sem.at[1]),
        pltpu.make_async_copy(evals_hbm, evals, local_sem.at[2]),
        pltpu.make_async_copy(tids_hbm, ids.at[core], local_sem.at[3]),
    ]
    for copy in small:
        copy.start()
    own_columns = pl.ds(pl.multiple_of(core * BLOCK, BLOCK), BLOCK)
    own_basis = pltpu.make_async_copy(eigen_hbm.at[0, :, core], basis.at[:, :, own_columns], local_sem.at[4])
    own_basis.start()
    own_rows = pl.ds(pl.multiple_of(core * ROWS, ROWS), ROWS)
    for index in range(CHIPS):
        kept = pl.ds(pl.multiple_of((index * CORES + core) * BLOCK, BLOCK), BLOCK)
        to_columns = pl.ds((index % SIDE) * BLOCK, BLOCK)
        pltpu.make_async_copy(
            train_hbm.at[0, :, kept], train.at[index // SIDE, own_rows, to_columns], train_sem.at[0]
        ).start()

    for copy in small:
        copy.wait()
    pick = (lax.broadcasted_iota(jnp.int32, (256, QUERIES), 0) == qids[...]).astype(F32).astype(BF16)
    message[...] = dot(pick, pool[...], 0, 0).astype(BF16)
    own_features = pl.ds(pl.multiple_of(x * BLOCK, BLOCK), BLOCK)
    gathered[z_hi, :, own_features] = message[...]
    all_evals[chip] = evals[...]

    pl.semaphore_wait(barrier, 15 + 31)

    send_basis = remote(
        eigen_hbm.at[0, :, 1 - core], basis.at[:, :, own_columns], basis_sem.at[0], basis_sem.at[1], layer, twin
    )
    send_basis.start()
    for dz, dx in others:
        target = peer(dz, dx) * CORES + core
        remote(
            message, gathered.at[z_hi, :, own_features], gather_sem.at[0], gather_sem.at[1 + dz], layer, target
        ).start()
    for dz, dx in others:
        target = peer(dz, dx) * CORES + core
        remote(evals, all_evals.at[chip], evals_sem.at[0], evals_sem.at[1], layer, target).start()
    send_ids = remote(ids.at[core], ids.at[core], ids_sem.at[0], ids_sem.at[1], layer, twin)
    send_ids.start()
    for index in range(CHIPS):
        sent = pl.ds(pl.multiple_of((index * CORES + 1 - core) * BLOCK, BLOCK), BLOCK)
        to_columns = pl.ds((index % SIDE) * BLOCK, BLOCK)
        remote(
            train_hbm.at[0, :, sent], train.at[index // SIDE, own_rows, to_columns],
            train_sem.at[1], train_sem.at[2], layer, twin,
        ).start()

    send_ids.wait()
    hit_0, codes_0 = owner_order(ids[0])
    hit_1, codes_1 = owner_order(ids[1])
    codes[0] = codes_0
    codes[1] = codes_1
    all_codes[chip, 0] = codes_0
    all_codes[chip, 1] = codes_1

    own_basis.wait()
    send_basis.wait()

    def row_of(dz):
        return lax.rem(z_hi + (SIDE - dz), SIDE)

    rotated = jnp.zeros((QUERIES, CORES * BLOCK), F32)
    for dz in (0, 1, 3, 2):
        row = row_of(dz)
        if dz == 0:
            drain(gathered.at[0, :, pl.ds(0, 3 * BLOCK)], gather_sem.at[1])
        else:
            drain(gathered.at[0], gather_sem.at[1 + dz])
        rows = basis[pl.ds(row * SIDE, SIDE)].reshape(SIDE * BLOCK, CORES * BLOCK)
        rotated += dot(gathered[row], rows, 1, 0)
    drain(all_evals.at[pl.ds(0, 15)], evals_sem.at[1])
    total = jnp.sum(all_evals[...][:, 0, :], keepdims=True)
    pair_send[0:QUERIES, :] = rotated
    pair_lane = lax.broadcasted_iota(jnp.int32, (8, CORES * BLOCK), 1)
    pair_row = lax.broadcasted_iota(jnp.int32, (8, CORES * BLOCK), 0)
    mine = pair_lane // BLOCK == core
    wide = jnp.concatenate([evals[...], evals[...]], axis=1)
    pair_send[QUERIES : QUERIES + 8, :] = jnp.where(
        pair_row == 0, jnp.where(mine, wide, 0.0), jnp.where(pair_row == 1, total, 0.0)
    )
    send_pair = remote(pair_send, pair_recv, pair_sem.at[0], pair_sem.at[1], layer, twin)
    send_pair.start()
    for dz, dx in others:
        target = peer(dz, dx) * CORES + core
        remote(codes, all_codes.at[chip], codes_sem.at[0], codes_sem.at[1], layer, target).start()
    send_pair.wait()
    both = pair_send[...] + pair_recv[...]
    damping = 0.1 * both[QUERIES + 1 : QUERIES + 2, :] / WIDTH
    damped = (both[0:QUERIES, :] / (both[QUERIES : QUERIES + 1, :] + damping)).astype(BF16)

    for dz, dx in others:
        target = peer(dz, dx)
        back_send[target] = dot(damped, basis[target], 1, 1).astype(BF16)
        remote(
            back_send.at[target], back_recv.at[chip], back_sem.at[0], back_sem.at[1 + dz], layer, target * CORES + core
        ).start()
    precond_sum = dot(damped, basis[chip], 1, 1)
    back_recv[chip] = jnp.zeros((QUERIES, BLOCK), BF16)

    for sem in range(3):
        drain(train.at[:, pl.ds(0, ROWS), :], train_sem.at[sem])
    for index in range(SIDE):
        sorted_train[index, 0:ROWS, :] = dot(hit_0, train[index, 0:ROWS, :], 1, 0).astype(BF16)
        sorted_train[index, ROWS : 2 * ROWS, :] = dot(hit_1, train[index, ROWS : 2 * ROWS, :], 1, 0).astype(BF16)

    for dz in (0, 1, 3, 2):
        drain(back_recv.at[pl.ds(0, 3 if dz == 0 else 4)], back_sem.at[1 + dz])
        precond_sum += jnp.sum(back_recv[pl.ds(row_of(dz) * SIDE, SIDE)].astype(F32), axis=0)
    piece[...] = precond_sum.astype(BF16)
    precond[z_hi, :, own_features] = piece[...]
    for dz, dx in others:
        target = peer(dz, dx) * CORES + core
        remote(
            piece, precond.at[z_hi, :, own_features], precond_sem.at[0], precond_sem.at[1 + dz], layer, target
        ).start()

    total_scores = jnp.zeros((ROWS, BLOCK), F32)
    nothing = jnp.zeros((QUERIES, SIDE * BLOCK), BF16)
    for dz in (0, 1, 3, 2):
        row = row_of(dz)
        if dz == 0:
            drain(precond.at[0, :, pl.ds(0, 3 * BLOCK)], precond_sem.at[1])
        else:
            drain(precond.at[0], precond_sem.at[1 + dz])
        queries = precond[row]
        total_scores += dot(sorted_train[row, 0:ROWS, :], jnp.concatenate([queries, nothing], axis=0), 1, 1)
        total_scores += dot(sorted_train[row, ROWS : 2 * ROWS, :], jnp.concatenate([nothing, queries], axis=0), 1, 1)
    scores[...] = total_scores
    mine_at = layer * CORES + core
    for step in LAYER_STEPS:
        other = lax.rem(layer + step, LAYERS)
        for flip in range(CORES):
            if step == 0 and flip == 0:
                continue
            to_core = core if flip == 0 else 1 - core
            rows = pl.ds(pl.multiple_of((other * CORES + to_core) * 8, 8), 8)
            remote(
                scores.at[rows, :], layer_recv.at[mine_at], layer_sem.at[0], layer_sem.at[1],
                other, chip * CORES + to_core,
            ).start()
    layer_recv[mine_at] = scores[pl.ds(pl.multiple_of(mine_at * 8, 8), 8), :]

    drain(all_codes.at[pl.ds(0, 15)], codes_sem.at[1])
    rank = lax.broadcasted_iota(jnp.int32, (CHIPS, 8, ROWS), 1)
    lane = lax.broadcasted_iota(jnp.int32, (CHIPS, 8, ROWS), 2).astype(F32)
    put = []
    for source in range(CORES):
        code = all_codes[:, source]
        place = code // ROWS
        slot = (code - place * ROWS).astype(F32)
        wanted = jnp.sum(jnp.where(place - 8 * blk == rank, slot, 0.0), axis=2, keepdims=True)
        put.append((wanted == lane).astype(F32).reshape(BLOCK, ROWS).astype(BF16))

    drain(layer_recv.at[pl.ds(0, 31)], layer_sem.at[1])
    tile[...] = jnp.sum(layer_recv[...], axis=0)

    owner = layer * CORES + core
    for step in LAYER_STEPS:
        if step == 0:
            continue
        other = lax.rem(layer + step, LAYERS)
        remote(tile, final.at[chip], final_sem.at[0], final_sem.at[1], other, owner).start()

    @pl.when(layer != chip)
    def _():
        remote(tile, final.at[chip], final_sem.at[2], final_sem.at[1], layer, owner).start()

    @pl.when(layer == chip)
    def _():
        pltpu.make_async_copy(tile, final.at[chip], final_sem.at[1]).start()

    drain(final, final_sem.at[1])
    values = final[...].reshape(BLOCK, BLOCK)
    placed_0 = jnp.zeros((BLOCK, ROWS), F32)
    placed_1 = jnp.zeros((BLOCK, ROWS), F32)
    for term in split3(values):
        placed_0 += dot(term, put[0], 0, 0)
        placed_1 += dot(term, put[1], 0, 0)
    out_ref[...] = placed_0[0:QUERIES, :] + placed_1[QUERIES : 2 * QUERIES, :]

    for _ in range(5):
        drain(gathered.at[0, :, pl.ds(0, 3 * BLOCK)], gather_sem.at[0])
    drain(all_evals.at[pl.ds(0, 15)], evals_sem.at[0])
    drain(all_codes.at[pl.ds(0, 15)], codes_sem.at[0])
    drain(back_recv.at[pl.ds(0, 15)], back_sem.at[0])
    for _ in range(5):
        drain(precond.at[0, :, pl.ds(0, 3 * BLOCK)], precond_sem.at[0])
    drain(layer_recv.at[pl.ds(0, 31)], layer_sem.at[0])
    drain(final.at[pl.ds(0, 15)], final_sem.at[0])

    @pl.when(layer != chip)
    def _():
        drain(tile, final_sem.at[2])


def on_device(query_pool, query_ids, eigenbasis, eigenvalues, train_grads, train_ids):
    return pl.pallas_call(
        kernel,
        out_shape=jax.ShapeDtypeStruct((QUERIES, ROWS), F32),
        in_specs=[pl.BlockSpec(memory_space=pl.ANY)] * 6,
        out_specs=pl.BlockSpec(memory_space=pltpu.VMEM),
        scratch_shapes=[
            pltpu.VMEM((256, BLOCK), BF16),
            pltpu.VMEM((1, QUERIES), jnp.int32),
            pltpu.VMEM((1, BLOCK), F32),
            pltpu.VMEM((CORES, 1, ROWS), jnp.int32),
            pltpu.VMEM((CHIPS, BLOCK, CORES * BLOCK), BF16),
            pltpu.VMEM((SIDE, CORES * ROWS, SIDE * BLOCK), BF16),
            pltpu.VMEM((SIDE, CORES * ROWS, SIDE * BLOCK), BF16),
            pltpu.VMEM((SIDE, QUERIES, SIDE * BLOCK), BF16),
            pltpu.VMEM((QUERIES, BLOCK), BF16),
            pltpu.VMEM((CHIPS, 1, BLOCK), F32),
            pltpu.VMEM((QUERIES + 8, CORES * BLOCK), F32),
            pltpu.VMEM((QUERIES + 8, CORES * BLOCK), F32),
            pltpu.VMEM((CORES, 1, ROWS), jnp.int32),
            pltpu.VMEM((CHIPS, CORES, 1, ROWS), jnp.int32),
            pltpu.VMEM((CHIPS, QUERIES, BLOCK), BF16),
            pltpu.VMEM((CHIPS, QUERIES, BLOCK), BF16),
            pltpu.VMEM((QUERIES, BLOCK), BF16),
            pltpu.VMEM((SIDE, QUERIES, SIDE * BLOCK), BF16),
            pltpu.VMEM((ROWS, BLOCK), F32),
            pltpu.VMEM((CORES * LAYERS, 8, BLOCK), F32),
            pltpu.VMEM((8, BLOCK), F32),
            pltpu.VMEM((CHIPS, 8, BLOCK), F32),
            pltpu.SemaphoreType.DMA((5,)),
            pltpu.SemaphoreType.DMA((2,)),
            pltpu.SemaphoreType.DMA((3,)),
            pltpu.SemaphoreType.DMA((2,)),
            pltpu.SemaphoreType.DMA((5,)),
            pltpu.SemaphoreType.DMA((2,)),
            pltpu.SemaphoreType.DMA((2,)),
            pltpu.SemaphoreType.DMA((2,)),
            pltpu.SemaphoreType.DMA((5,)),
            pltpu.SemaphoreType.DMA((5,)),
            pltpu.SemaphoreType.DMA((2,)),
            pltpu.SemaphoreType.DMA((3,)),
        ],
        compiler_params=pltpu.CompilerParams(
            collective_id=0, has_side_effects=True, vmem_limit_bytes=40 * 1024 * 1024
        ),
        cost_estimate=pl.CostEstimate(flops=600_000_000, bytes_accessed=4_000_000, transcendentals=0),
    )(
        *[
            pltpu.with_memory_space_constraint(array, pltpu.HBM)
            for array in (
                query_pool,
                query_ids.reshape(1, QUERIES),
                eigenbasis.reshape(1, CHIPS, CORES, BLOCK, BLOCK),
                eigenvalues,
                train_grads,
                train_ids.reshape(1, ROWS),
            )
        ]
    )


def solution(mesh):
    in_specs = (
        P("layer", None, "blk"),
        P(),
        P("layer", None, "blk"),
        P("layer", "blk"),
        P("layer", "blk", None),
        P("blk"),
    )
    out_specs = P(None, "blk")
    return jax.shard_map(
        on_device, mesh=mesh, in_specs=in_specs, out_specs=out_specs, check_vma=False
    )
```

```python
import jax
import jax.numpy as jnp
from jax import lax
from jax.experimental import pallas as pl
from jax.experimental.pallas import tpu as pltpu
from jax.sharding import PartitionSpec as P

WIDTH = 4096
QUERIES = 64
PARTS = 2
PART = QUERIES // PARTS
LAG = 0
LAYERS = 16
CHIPS = 16
CORES = 2
SIDE = 4
LAYER_STEPS = (8, 9, 7, 10, 6, 11, 5, 12, 4, 13, 3, 14, 2, 15, 1, 0)
BLOCK = 128
ROWS = 256
MESH = pl.DeviceIdType.MESH
F32 = jnp.float32
BF16 = jnp.bfloat16


def split3(value):
    first = value.astype(BF16)
    rest = value - first.astype(F32)
    second = rest.astype(BF16)
    third = (rest - second.astype(F32)).astype(BF16)
    return first, second, third


def dot(a, b, a_dim, b_dim):
    return lax.dot_general(a, b, (((a_dim,), (b_dim,)), ((), ())), preferred_element_type=F32)


def owner_order(ids):
    owner = ids // ROWS
    slot = ids - owner * ROWS
    member = (lax.broadcasted_iota(jnp.int32, (32, ROWS), 0) == owner).astype(F32)
    before = lax.broadcasted_iota(jnp.int32, (ROWS, ROWS), 0) < lax.broadcasted_iota(jnp.int32, (ROWS, ROWS), 1)
    counts = dot(member.astype(BF16), before.astype(F32).astype(BF16), 1, 0)
    rank = jnp.sum(member * counts, axis=0, keepdims=True)
    place = owner * 8 + rank.astype(jnp.int32)
    hit = lax.broadcasted_iota(jnp.int32, (ROWS, ROWS), 0) == place
    return hit.astype(F32).astype(BF16), place * ROWS + slot


def kernel(
    pool_hbm, qids_hbm, eigen_hbm, evals_hbm, train_hbm, tids_hbm, out_ref,
    pool, qids, evals, ids, basis, train, sorted_train, gathered, message, all_evals, pair_evals, pair_send, pair_recv,
    codes, all_codes, back_send, back_recv, piece, precond, scores, layer_recv, tile, final,
    local_sem, basis_sem, train_sem, ids_sem, gather_sem, evals_sem, pair_sem, codes_sem, back_sem, precond_sem,
    layer_sem, final_sem,
):
    layer = lax.axis_index("layer")
    blk = lax.axis_index("blk")
    chip = blk // CORES
    core = blk - chip * CORES
    z_hi = chip // SIDE
    x = chip - z_hi * SIDE
    twin = chip * CORES + (1 - core)

    others = [
        (2, 2), (1, 2), (3, 2), (2, 1), (2, 3), (1, 1), (3, 3), (2, 0), (1, 3), (3, 1), (1, 0), (3, 0), (0, 2), (0, 1), (0, 3)
    ]

    def peer(dz, dx):
        return lax.rem(z_hi + dz, SIDE) * SIDE + lax.rem(x + dx, SIDE)

    def remote(src, dst, send, recv, to_layer, to_blk):
        return pltpu.make_async_remote_copy(
            src_ref=src, dst_ref=dst, send_sem=send, recv_sem=recv,
            device_id=(to_layer, to_blk), device_id_type=MESH,
        )

    def drain(ref, sem):
        pltpu.make_async_copy(ref, ref, sem).wait()

    barrier = pltpu.get_barrier_semaphore()
    for dz, dx in others:
        pl.semaphore_signal(barrier, inc=1, device_id=(layer, peer(dz, dx) * CORES + core), device_id_type=MESH)
    for step in range(LAYERS):
        other = lax.rem(layer + step, LAYERS)
        if step > 0:
            pl.semaphore_signal(barrier, inc=1, device_id=(other, blk), device_id_type=MESH)
        pl.semaphore_signal(barrier, inc=1, device_id=(other, twin), device_id_type=MESH)

    small = [
        pltpu.make_async_copy(pool_hbm.at[0], pool, local_sem.at[0]),
        pltpu.make_async_copy(qids_hbm, qids, local_sem.at[1]),
        pltpu.make_async_copy(evals_hbm, evals, local_sem.at[2]),
        pltpu.make_async_copy(tids_hbm, ids.at[core], local_sem.at[3]),
    ]
    for copy in small:
        copy.start()
    own_columns = pl.ds(pl.multiple_of(core * BLOCK, BLOCK), BLOCK)
    own_basis = pltpu.make_async_copy(eigen_hbm.at[0, :, core], basis.at[:, :, own_columns], local_sem.at[4])
    own_basis.start()
    own_rows = pl.ds(pl.multiple_of(core * ROWS, ROWS), ROWS)
    for index in range(CHIPS):
        kept = pl.ds(pl.multiple_of((index * CORES + core) * BLOCK, BLOCK), BLOCK)
        to_columns = pl.ds((index % SIDE) * BLOCK, BLOCK)
        pltpu.make_async_copy(
            train_hbm.at[0, :, kept], train.at[index // SIDE, own_rows, to_columns], train_sem.at[0]
        ).start()

    for copy in small:
        copy.wait()
    pick = (lax.broadcasted_iota(jnp.int32, (256, QUERIES), 0) == qids[...]).astype(F32).astype(BF16)
    message[...] = dot(pick, pool[...], 0, 0).astype(BF16).reshape(PARTS, PART, BLOCK)
    own_features = pl.ds(pl.multiple_of(x * BLOCK, BLOCK), BLOCK)
    gathered[:, z_hi, :, own_features] = message[...]
    all_evals[chip] = evals[...]

    pl.semaphore_wait(barrier, 15 + 31)

    for dz, dx in others:
        target = peer(dz, dx) * CORES + core
        remote(evals, all_evals.at[chip], evals_sem.at[0], evals_sem.at[1], layer, target).start()
    send_basis = remote(
        eigen_hbm.at[0, :, 1 - core], basis.at[:, :, own_columns], basis_sem.at[0], basis_sem.at[1], layer, twin
    )
    send_basis.start()
    for part in range(PARTS):
        for dz, dx in others:
            target = peer(dz, dx) * CORES + core
            remote(
                message.at[part], gathered.at[part, z_hi, :, own_features],
                gather_sem.at[0], gather_sem.at[1 + part * SIDE + dz], layer, target,
            ).start()
    send_ids = remote(ids.at[core], ids.at[core], ids_sem.at[0], ids_sem.at[1], layer, twin)
    send_ids.start()
    for index in range(CHIPS):
        sent = pl.ds(pl.multiple_of((index * CORES + 1 - core) * BLOCK, BLOCK), BLOCK)
        to_columns = pl.ds((index % SIDE) * BLOCK, BLOCK)
        remote(
            train_hbm.at[0, :, sent], train.at[index // SIDE, own_rows, to_columns],
            train_sem.at[1], train_sem.at[2], layer, twin,
        ).start()

    send_ids.wait()
    hit_0, codes_0 = owner_order(ids[0])
    hit_1, codes_1 = owner_order(ids[1])
    codes[0] = codes_0
    codes[1] = codes_1
    all_codes[chip, 0] = codes_0
    all_codes[chip, 1] = codes_1

    own_basis.wait()
    send_basis.wait()

    def row_of(dz):
        return lax.rem(z_hi + (SIDE - dz), SIDE)

    drain(all_evals.at[pl.ds(0, 15)], evals_sem.at[1])
    total = jnp.sum(all_evals[...][:, 0, :], keepdims=True)
    pair_lane = lax.broadcasted_iota(jnp.int32, (8, CORES * BLOCK), 1)
    pair_row = lax.broadcasted_iota(jnp.int32, (8, CORES * BLOCK), 0)
    mine = pair_lane // BLOCK == core
    wide = jnp.concatenate([evals[...], evals[...]], axis=1)
    pair_evals[0] = jnp.where(
        pair_row == 0, jnp.where(mine, wide, 0.0), jnp.where(pair_row == 1, total, 0.0)
    )
    send_evals = remote(pair_evals.at[0], pair_evals.at[1], evals_sem.at[2], evals_sem.at[3], layer, twin)
    send_evals.start()

    send_pair = []
    own_parts = []

    def rotate(part):
        rotated = jnp.zeros((PART, CORES * BLOCK), F32)
        for dz in (0, 1, 3, 2):
            row = row_of(dz)
            arrival = gather_sem.at[1 + part * SIDE + dz]
            if dz == 0:
                drain(gathered.at[part, 0, :, pl.ds(0, 3 * BLOCK)], arrival)
            else:
                drain(gathered.at[part, 0], arrival)
            rows = basis[pl.ds(row * SIDE, SIDE)].reshape(SIDE * BLOCK, CORES * BLOCK)
            rotated += dot(gathered[part, row], rows, 1, 0)
        pair_send[part] = rotated
        send_pair.append(
            remote(pair_send.at[part], pair_recv.at[part], pair_sem.at[0], pair_sem.at[1 + part], layer, twin)
        )
        send_pair[part].start()

    def send_back(part):
        send_pair[part].wait_recv()
        damped = ((pair_send[part] + pair_recv[part]) / divisor).astype(BF16)
        for dz in (2, 1, 3, 0):
            row = lax.rem(z_hi + dz, SIDE)
            rows = basis[pl.ds(row * SIDE, SIDE)].reshape(SIDE * BLOCK, CORES * BLOCK)
            back_send[part, row] = dot(damped, rows, 1, 1).astype(BF16)
            for dx in (2, 1, 3, 0):
                if dz == 0 and dx == 0:
                    continue
                column = lax.rem(x + dx, SIDE)
                block = pl.ds(pl.multiple_of(column * BLOCK, BLOCK), BLOCK)
                remote(
                    back_send.at[part, row, :, block], back_recv.at[part, chip],
                    back_sem.at[0], back_sem.at[1 + part * SIDE + dz], layer, (row * SIDE + column) * CORES + core,
                ).start()
        own_parts.append(dot(damped, basis[chip], 1, 1))
        back_recv[part, chip] = jnp.zeros((PART, BLOCK), BF16)

    for part in range(PARTS + LAG):
        if part < PARTS:
            rotate(part)
        if part == 0:
            send_evals.wait()
            both = pair_evals[0] + pair_evals[1]
            divisor = both[0:1, :] + 0.1 * both[1:2, :] / WIDTH
        if part >= LAG:
            send_back(part - LAG)
    for dz, dx in others:
        target = peer(dz, dx) * CORES + core
        remote(codes, all_codes.at[chip], codes_sem.at[0], codes_sem.at[1], layer, target).start()

    for sem in range(3):
        drain(train.at[:, pl.ds(0, ROWS), :], train_sem.at[sem])
    for index in range(SIDE):
        sorted_train[index, 0:ROWS, :] = dot(hit_0, train[index, 0:ROWS, :], 1, 0).astype(BF16)
        sorted_train[index, ROWS : 2 * ROWS, :] = dot(hit_1, train[index, ROWS : 2 * ROWS, :], 1, 0).astype(BF16)

    for part in range(PARTS):
        precond_sum = own_parts[part]
        for dz in (0, 1, 3, 2):
            drain(back_recv.at[part, pl.ds(0, 3 if dz == 0 else 4)], back_sem.at[1 + part * SIDE + dz])
            precond_sum += jnp.sum(back_recv[part, pl.ds(row_of(dz) * SIDE, SIDE)].astype(F32), axis=0)
        piece[part] = precond_sum.astype(BF16)
        precond[z_hi, pl.ds(part * PART, PART), own_features] = piece[part]
        for dz, dx in others:
            target = peer(dz, dx) * CORES + core
            remote(
                piece.at[part], precond.at[z_hi, pl.ds(part * PART, PART), own_features],
                precond_sem.at[0], precond_sem.at[1 + part * SIDE + dz], layer, target,
            ).start()

    total_scores = jnp.zeros((ROWS, BLOCK), F32)
    nothing = jnp.zeros((QUERIES, SIDE * BLOCK), BF16)
    for dz in (0, 1, 3, 2):
        row = row_of(dz)
        for part in range(PARTS):
            arrival = precond_sem.at[1 + part * SIDE + dz]
            if dz == 0:
                drain(precond.at[0, pl.ds(0, PART), pl.ds(0, 3 * BLOCK)], arrival)
            else:
                drain(precond.at[0, pl.ds(0, PART)], arrival)
        queries = precond[row]
        total_scores += dot(sorted_train[row, 0:ROWS, :], jnp.concatenate([queries, nothing], axis=0), 1, 1)
        total_scores += dot(sorted_train[row, ROWS : 2 * ROWS, :], jnp.concatenate([nothing, queries], axis=0), 1, 1)
    scores[...] = total_scores
    mine_at = layer * CORES + core
    for step in LAYER_STEPS:
        other = lax.rem(layer + step, LAYERS)
        for flip in range(CORES):
            if step == 0 and flip == 0:
                continue
            to_core = core if flip == 0 else 1 - core
            rows = pl.ds(pl.multiple_of((other * CORES + to_core) * 8, 8), 8)
            remote(
                scores.at[rows, :], layer_recv.at[mine_at], layer_sem.at[0], layer_sem.at[1],
                other, chip * CORES + to_core,
            ).start()
    layer_recv[mine_at] = scores[pl.ds(pl.multiple_of(mine_at * 8, 8), 8), :]

    drain(all_codes.at[pl.ds(0, 15)], codes_sem.at[1])
    rank = lax.broadcasted_iota(jnp.int32, (CHIPS, 8, ROWS), 1)
    lane = lax.broadcasted_iota(jnp.int32, (CHIPS, 8, ROWS), 2).astype(F32)
    put = []
    for source in range(CORES):
        code = all_codes[:, source]
        place = code // ROWS
        slot = (code - place * ROWS).astype(F32)
        wanted = jnp.sum(jnp.where(place - 8 * blk == rank, slot, 0.0), axis=2, keepdims=True)
        put.append((wanted == lane).astype(F32).reshape(BLOCK, ROWS).astype(BF16))

    drain(layer_recv.at[pl.ds(0, 31)], layer_sem.at[1])
    tile[...] = jnp.sum(layer_recv[...], axis=0)

    owner = layer * CORES + core
    for step in LAYER_STEPS:
        if step == 0:
            continue
        other = lax.rem(layer + step, LAYERS)
        remote(tile, final.at[chip], final_sem.at[0], final_sem.at[1], other, owner).start()

    @pl.when(layer != chip)
    def _():
        remote(tile, final.at[chip], final_sem.at[2], final_sem.at[1], layer, owner).start()

    @pl.when(layer == chip)
    def _():
        pltpu.make_async_copy(tile, final.at[chip], final_sem.at[1]).start()

    drain(final, final_sem.at[1])
    values = final[...].reshape(BLOCK, BLOCK)
    placed_0 = jnp.zeros((BLOCK, ROWS), F32)
    placed_1 = jnp.zeros((BLOCK, ROWS), F32)
    for term in split3(values):
        placed_0 += dot(term, put[0], 0, 0)
        placed_1 += dot(term, put[1], 0, 0)
    out_ref[...] = placed_0[0:QUERIES, :] + placed_1[QUERIES : 2 * QUERIES, :]

    for _ in range(5):
        drain(gathered.at[:, 0, :, pl.ds(0, 3 * BLOCK)], gather_sem.at[0])
    drain(pair_send, pair_sem.at[0])
    drain(all_evals.at[pl.ds(0, 15)], evals_sem.at[0])
    drain(all_codes.at[pl.ds(0, 15)], codes_sem.at[0])
    drain(back_recv.at[:, pl.ds(0, 15)], back_sem.at[0])
    for _ in range(5):
        drain(precond.at[0, :, pl.ds(0, 3 * BLOCK)], precond_sem.at[0])
    drain(layer_recv.at[pl.ds(0, 31)], layer_sem.at[0])
    drain(final.at[pl.ds(0, 15)], final_sem.at[0])

    @pl.when(layer != chip)
    def _():
        drain(tile, final_sem.at[2])


def on_device(query_pool, query_ids, eigenbasis, eigenvalues, train_grads, train_ids):
    return pl.pallas_call(
        kernel,
        out_shape=jax.ShapeDtypeStruct((QUERIES, ROWS), F32),
        in_specs=[pl.BlockSpec(memory_space=pl.ANY)] * 6,
        out_specs=pl.BlockSpec(memory_space=pltpu.VMEM),
        scratch_shapes=[
            pltpu.VMEM((256, BLOCK), BF16),
            pltpu.VMEM((1, QUERIES), jnp.int32),
            pltpu.VMEM((1, BLOCK), F32),
            pltpu.VMEM((CORES, 1, ROWS), jnp.int32),
            pltpu.VMEM((CHIPS, BLOCK, CORES * BLOCK), BF16),
            pltpu.VMEM((SIDE, CORES * ROWS, SIDE * BLOCK), BF16),
            pltpu.VMEM((SIDE, CORES * ROWS, SIDE * BLOCK), BF16),
            pltpu.VMEM((PARTS, SIDE, PART, SIDE * BLOCK), BF16),
            pltpu.VMEM((PARTS, PART, BLOCK), BF16),
            pltpu.VMEM((CHIPS, 1, BLOCK), F32),
            pltpu.VMEM((2, 8, CORES * BLOCK), F32),
            pltpu.VMEM((PARTS, PART, CORES * BLOCK), F32),
            pltpu.VMEM((PARTS, PART, CORES * BLOCK), F32),
            pltpu.VMEM((CORES, 1, ROWS), jnp.int32),
            pltpu.VMEM((CHIPS, CORES, 1, ROWS), jnp.int32),
            pltpu.VMEM((PARTS, SIDE, PART, SIDE * BLOCK), BF16),
            pltpu.VMEM((PARTS, CHIPS, PART, BLOCK), BF16),
            pltpu.VMEM((PARTS, PART, BLOCK), BF16),
            pltpu.VMEM((SIDE, QUERIES, SIDE * BLOCK), BF16),
            pltpu.VMEM((ROWS, BLOCK), F32),
            pltpu.VMEM((CORES * LAYERS, 8, BLOCK), F32),
            pltpu.VMEM((8, BLOCK), F32),
            pltpu.VMEM((CHIPS, 8, BLOCK), F32),
            pltpu.SemaphoreType.DMA((5,)),
            pltpu.SemaphoreType.DMA((2,)),
            pltpu.SemaphoreType.DMA((3,)),
            pltpu.SemaphoreType.DMA((2,)),
            pltpu.SemaphoreType.DMA((1 + PARTS * SIDE,)),
            pltpu.SemaphoreType.DMA((4,)),
            pltpu.SemaphoreType.DMA((1 + PARTS,)),
            pltpu.SemaphoreType.DMA((2,)),
            pltpu.SemaphoreType.DMA((1 + PARTS * SIDE,)),
            pltpu.SemaphoreType.DMA((1 + PARTS * SIDE,)),
            pltpu.SemaphoreType.DMA((2,)),
            pltpu.SemaphoreType.DMA((3,)),
        ],
        compiler_params=pltpu.CompilerParams(
            collective_id=0, has_side_effects=True, vmem_limit_bytes=40 * 1024 * 1024
        ),
        cost_estimate=pl.CostEstimate(flops=600_000_000, bytes_accessed=4_000_000, transcendentals=0),
    )(
        *[
            pltpu.with_memory_space_constraint(array, pltpu.HBM)
            for array in (
                query_pool,
                query_ids.reshape(1, QUERIES),
                eigenbasis.reshape(1, CHIPS, CORES, BLOCK, BLOCK),
                eigenvalues,
                train_grads,
                train_ids.reshape(1, ROWS),
            )
        ]
    )


def solution(mesh):
    in_specs = (
        P("layer", None, "blk"),
        P(),
        P("layer", None, "blk"),
        P("layer", "blk"),
        P("layer", "blk", None),
        P("blk"),
    )
    out_specs = P(None, "blk")
    return jax.shard_map(
        on_device, mesh=mesh, in_specs=in_specs, out_specs=out_specs, check_vma=False
    )
```

```python
import jax
import jax.numpy as jnp
from jax import lax
from jax.experimental import pallas as pl
from jax.experimental.pallas import tpu as pltpu
from jax.sharding import PartitionSpec as P

WIDTH = 4096
QUERIES = 64
PARTS = ((0, 32), (32, 32))
LAG = 0
LAYERS = 16
CHIPS = 16
CORES = 2
SIDE = 4
LAYER_STEPS = (8, 9, 7, 10, 6, 11, 5, 12, 4, 13, 3, 14, 2, 15, 1, 0)
BLOCK = 128
ROWS = 256
MESH = pl.DeviceIdType.MESH
F32 = jnp.float32
BF16 = jnp.bfloat16


def split3(value):
    first = value.astype(BF16)
    rest = value - first.astype(F32)
    second = rest.astype(BF16)
    third = (rest - second.astype(F32)).astype(BF16)
    return first, second, third


def dot(a, b, a_dim, b_dim):
    return lax.dot_general(a, b, (((a_dim,), (b_dim,)), ((), ())), preferred_element_type=F32)


def owner_order(ids):
    owner = ids // ROWS
    slot = ids - owner * ROWS
    member = (lax.broadcasted_iota(jnp.int32, (32, ROWS), 0) == owner).astype(F32)
    before = lax.broadcasted_iota(jnp.int32, (ROWS, ROWS), 0) < lax.broadcasted_iota(jnp.int32, (ROWS, ROWS), 1)
    counts = dot(member.astype(BF16), before.astype(F32).astype(BF16), 1, 0)
    rank = jnp.sum(member * counts, axis=0, keepdims=True)
    place = owner * 8 + rank.astype(jnp.int32)
    hit = lax.broadcasted_iota(jnp.int32, (ROWS, ROWS), 0) == place
    return hit.astype(F32).astype(BF16), place * ROWS + slot


def kernel(
    pool_hbm, qids_hbm, eigen_hbm, evals_hbm, train_hbm, tids_hbm, out_ref,
    pool, qids, evals, ids, basis, train, sorted_train, gathered, message, all_evals, pair_evals, pair_send, pair_recv,
    codes, all_codes, back_send, back_recv, piece, precond, scores, layer_recv, tile, final,
    local_sem, basis_sem, train_sem, ids_sem, gather_sem, evals_sem, pair_sem, codes_sem, back_sem, precond_sem,
    layer_sem, final_sem,
):
    layer = lax.axis_index("layer")
    blk = lax.axis_index("blk")
    chip = blk // CORES
    core = blk - chip * CORES
    z_hi = chip // SIDE
    x = chip - z_hi * SIDE
    twin = chip * CORES + (1 - core)

    others = [
        (2, 2), (1, 2), (3, 2), (2, 1), (2, 3), (1, 1), (3, 3), (2, 0), (1, 3), (3, 1), (1, 0), (3, 0), (0, 2), (0, 1), (0, 3)
    ]

    def peer(dz, dx):
        return lax.rem(z_hi + dz, SIDE) * SIDE + lax.rem(x + dx, SIDE)

    def remote(src, dst, send, recv, to_layer, to_blk):
        return pltpu.make_async_remote_copy(
            src_ref=src, dst_ref=dst, send_sem=send, recv_sem=recv,
            device_id=(to_layer, to_blk), device_id_type=MESH,
        )

    def drain(ref, sem):
        pltpu.make_async_copy(ref, ref, sem).wait()

    barrier = pltpu.get_barrier_semaphore()
    for dz, dx in others:
        pl.semaphore_signal(barrier, inc=1, device_id=(layer, peer(dz, dx) * CORES + core), device_id_type=MESH)
    for step in range(LAYERS):
        other = lax.rem(layer + step, LAYERS)
        if step > 0:
            pl.semaphore_signal(barrier, inc=1, device_id=(other, blk), device_id_type=MESH)
        pl.semaphore_signal(barrier, inc=1, device_id=(other, twin), device_id_type=MESH)

    small = [
        pltpu.make_async_copy(pool_hbm.at[0], pool, local_sem.at[0]),
        pltpu.make_async_copy(qids_hbm, qids, local_sem.at[1]),
        pltpu.make_async_copy(evals_hbm, evals, local_sem.at[2]),
        pltpu.make_async_copy(tids_hbm, ids.at[core], local_sem.at[3]),
    ]
    for copy in small:
        copy.start()
    own_columns = pl.ds(pl.multiple_of(core * BLOCK, BLOCK), BLOCK)
    own_basis = pltpu.make_async_copy(eigen_hbm.at[0, :, core], basis.at[:, :, own_columns], local_sem.at[4])
    own_basis.start()
    own_rows = pl.ds(pl.multiple_of(core * ROWS, ROWS), ROWS)
    for index in range(CHIPS):
        kept = pl.ds(pl.multiple_of((index * CORES + core) * BLOCK, BLOCK), BLOCK)
        to_columns = pl.ds((index % SIDE) * BLOCK, BLOCK)
        pltpu.make_async_copy(
            train_hbm.at[0, :, kept], train.at[index // SIDE, own_rows, to_columns], train_sem.at[0]
        ).start()

    for copy in small:
        copy.wait()
    pick = (lax.broadcasted_iota(jnp.int32, (256, QUERIES), 0) == qids[...]).astype(F32).astype(BF16)
    message[...] = dot(pick, pool[...], 0, 0).astype(BF16)
    own_features = pl.ds(pl.multiple_of(x * BLOCK, BLOCK), BLOCK)
    gathered[z_hi, :, own_features] = message[...]
    all_evals[chip] = evals[...]

    pl.semaphore_wait(barrier, 15 + 31)

    for dz, dx in others:
        target = peer(dz, dx) * CORES + core
        remote(evals, all_evals.at[chip], evals_sem.at[0], evals_sem.at[1], layer, target).start()
    send_basis = remote(
        eigen_hbm.at[0, :, 1 - core], basis.at[:, :, own_columns], basis_sem.at[0], basis_sem.at[1], layer, twin
    )
    send_basis.start()
    for part, (first, count) in enumerate(PARTS):
        rows = pl.ds(first, count)
        for dz, dx in others:
            target = peer(dz, dx) * CORES + core
            remote(
                message.at[rows], gathered.at[z_hi, rows, own_features],
                gather_sem.at[0], gather_sem.at[1 + part * SIDE + dz], layer, target,
            ).start()
    send_ids = remote(ids.at[core], ids.at[core], ids_sem.at[0], ids_sem.at[1], layer, twin)
    send_ids.start()
    send_ids.wait()
    hit_0, codes_0 = owner_order(ids[0])
    hit_1, codes_1 = owner_order(ids[1])
    codes[0] = codes_0
    codes[1] = codes_1
    all_codes[chip, 0] = codes_0
    all_codes[chip, 1] = codes_1

    own_basis.wait()
    send_basis.wait()

    def row_of(dz):
        return lax.rem(z_hi + (SIDE - dz), SIDE)

    drain(all_evals.at[pl.ds(0, 15)], evals_sem.at[1])
    total = jnp.sum(all_evals[...][:, 0, :], keepdims=True)
    pair_lane = lax.broadcasted_iota(jnp.int32, (8, CORES * BLOCK), 1)
    pair_row = lax.broadcasted_iota(jnp.int32, (8, CORES * BLOCK), 0)
    mine = pair_lane // BLOCK == core
    wide = jnp.concatenate([evals[...], evals[...]], axis=1)
    pair_evals[0] = jnp.where(
        pair_row == 0, jnp.where(mine, wide, 0.0), jnp.where(pair_row == 1, total, 0.0)
    )
    send_evals = remote(pair_evals.at[0], pair_evals.at[1], evals_sem.at[2], evals_sem.at[3], layer, twin)
    send_evals.start()

    send_pair = []
    own_parts = []

    def rotate(part):
        first, count = PARTS[part]
        rotated = jnp.zeros((count, CORES * BLOCK), F32)
        for dz in (0, 1, 3, 2):
            row = row_of(dz)
            arrival = gather_sem.at[1 + part * SIDE + dz]
            if dz == 0:
                drain(gathered.at[0, pl.ds(0, count), pl.ds(0, 3 * BLOCK)], arrival)
            else:
                drain(gathered.at[0, pl.ds(0, count)], arrival)
            vectors = basis[pl.ds(row * SIDE, SIDE)].reshape(SIDE * BLOCK, CORES * BLOCK)
            rotated += dot(gathered[row, first : first + count, :], vectors, 1, 0)
        rows = pl.ds(first, count)
        pair_send[first : first + count, :] = rotated
        send_pair.append(
            remote(pair_send.at[rows], pair_recv.at[rows], pair_sem.at[0], pair_sem.at[1 + part], layer, twin)
        )
        send_pair[part].start()

    def send_back(part):
        first, count = PARTS[part]
        rows = pl.ds(first, count)
        send_pair[part].wait_recv()
        damped = ((pair_send[first : first + count, :] + pair_recv[first : first + count, :]) / divisor).astype(BF16)
        for dz in (2, 1, 3, 0):
            row = lax.rem(z_hi + dz, SIDE)
            vectors = basis[pl.ds(row * SIDE, SIDE)].reshape(SIDE * BLOCK, CORES * BLOCK)
            back_send[row, first : first + count, :] = dot(damped, vectors, 1, 1).astype(BF16)
            for dx in (2, 1, 3, 0):
                if dz == 0 and dx == 0:
                    continue
                column = lax.rem(x + dx, SIDE)
                block = pl.ds(pl.multiple_of(column * BLOCK, BLOCK), BLOCK)
                remote(
                    back_send.at[row, rows, block], back_recv.at[chip, rows],
                    back_sem.at[0], back_sem.at[1 + part * SIDE + dz], layer, (row * SIDE + column) * CORES + core,
                ).start()
        own_parts.append(dot(damped, basis[chip], 1, 1))
        back_recv[chip, first : first + count, :] = jnp.zeros((count, BLOCK), BF16)

    for part in range(len(PARTS) + LAG):
        if part < len(PARTS):
            rotate(part)
        if part == 0:
            send_evals.wait()
            both = pair_evals[0] + pair_evals[1]
            divisor = both[0:1, :] + 0.1 * both[1:2, :] / WIDTH
        if part >= LAG:
            send_back(part - LAG)

    for index in range(CHIPS):
        sent = pl.ds(pl.multiple_of((index * CORES + 1 - core) * BLOCK, BLOCK), BLOCK)
        to_columns = pl.ds((index % SIDE) * BLOCK, BLOCK)
        remote(
            train_hbm.at[0, :, sent], train.at[index // SIDE, own_rows, to_columns],
            train_sem.at[1], train_sem.at[2], layer, twin,
        ).start()

    for sem in range(3):
        drain(train.at[:, pl.ds(0, ROWS), :], train_sem.at[sem])
    for index in range(SIDE):
        sorted_train[index, 0:ROWS, :] = dot(hit_0, train[index, 0:ROWS, :], 1, 0).astype(BF16)
        sorted_train[index, ROWS : 2 * ROWS, :] = dot(hit_1, train[index, ROWS : 2 * ROWS, :], 1, 0).astype(BF16)

    for part, (first, count) in enumerate(PARTS):
        rows = pl.ds(first, count)
        precond_sum = own_parts[part]
        for dz in (0, 1, 3, 2):
            drain(back_recv.at[pl.ds(0, 3 if dz == 0 else 4), pl.ds(0, count)], back_sem.at[1 + part * SIDE + dz])
            arrived = back_recv[pl.ds(row_of(dz) * SIDE, SIDE), first : first + count, :]
            precond_sum += jnp.sum(arrived.astype(F32), axis=0)
        piece[first : first + count, :] = precond_sum.astype(BF16)
        precond[z_hi, first : first + count, own_features] = piece[first : first + count, :]
        for dz, dx in others:
            target = peer(dz, dx) * CORES + core
            remote(
                piece.at[rows], precond.at[z_hi, rows, own_features],
                precond_sem.at[0], precond_sem.at[1 + part * SIDE + dz], layer, target,
            ).start()

    by_query = jnp.zeros((QUERIES, CORES * ROWS), F32)
    for dz in (0, 1, 3, 2):
        row = row_of(dz)
        for part, (first, count) in enumerate(PARTS):
            arrival = precond_sem.at[1 + part * SIDE + dz]
            if dz == 0:
                drain(precond.at[0, pl.ds(0, count), pl.ds(0, 3 * BLOCK)], arrival)
            else:
                drain(precond.at[0, pl.ds(0, count)], arrival)
        by_query += dot(precond[row], sorted_train[row], 1, 1)
    by_core = jnp.concatenate([by_query[:, 0:ROWS], by_query[:, ROWS : 2 * ROWS]], axis=0)
    scores[...] = by_core.T
    mine_at = layer * CORES + core
    for step in LAYER_STEPS:
        other = lax.rem(layer + step, LAYERS)
        for flip in range(CORES):
            if step == 0 and flip == 0:
                continue
            to_core = core if flip == 0 else 1 - core
            rows = pl.ds(pl.multiple_of((other * CORES + to_core) * 8, 8), 8)
            remote(
                scores.at[rows, :], layer_recv.at[mine_at], layer_sem.at[0], layer_sem.at[1],
                other, chip * CORES + to_core,
            ).start()
    for dz, dx in others:
        target = peer(dz, dx) * CORES + core
        remote(codes, all_codes.at[chip], codes_sem.at[0], codes_sem.at[1], layer, target).start()
    layer_recv[mine_at] = scores[pl.ds(pl.multiple_of(mine_at * 8, 8), 8), :]

    drain(layer_recv.at[pl.ds(0, 31)], layer_sem.at[1])
    tile[...] = jnp.sum(layer_recv[...], axis=0)

    owner = layer * CORES + core
    for step in LAYER_STEPS:
        if step == 0:
            continue
        other = lax.rem(layer + step, LAYERS)
        remote(tile, final.at[chip], final_sem.at[0], final_sem.at[1], other, owner).start()

    @pl.when(layer != chip)
    def _():
        remote(tile, final.at[chip], final_sem.at[2], final_sem.at[1], layer, owner).start()

    @pl.when(layer == chip)
    def _():
        pltpu.make_async_copy(tile, final.at[chip], final_sem.at[1]).start()

    drain(all_codes.at[pl.ds(0, 15)], codes_sem.at[1])
    rank = lax.broadcasted_iota(jnp.int32, (CHIPS, 8, ROWS), 1)
    lane = lax.broadcasted_iota(jnp.int32, (CHIPS, 8, ROWS), 2).astype(F32)
    put = []
    for source in range(CORES):
        code = all_codes[:, source]
        place = code // ROWS
        slot = (code - place * ROWS).astype(F32)
        wanted = jnp.sum(jnp.where(place - 8 * blk == rank, slot, 0.0), axis=2, keepdims=True)
        put.append((wanted == lane).astype(F32).reshape(BLOCK, ROWS).astype(BF16))
    put = jnp.concatenate(put, axis=0)

    drain(final, final_sem.at[1])
    values = final[...].reshape(BLOCK, BLOCK).T
    values = jnp.concatenate([values[0:QUERIES, :], values[QUERIES : 2 * QUERIES, :]], axis=1)
    placed = dot(jnp.concatenate(split3(values), axis=0), put, 1, 0)
    placed = placed[0:QUERIES, :] + placed[QUERIES : 2 * QUERIES, :] + placed[2 * QUERIES : 3 * QUERIES, :]
    out_ref[...] = placed

    for _ in range(5):
        drain(gathered.at[0, :, pl.ds(0, 3 * BLOCK)], gather_sem.at[0])
    drain(pair_send, pair_sem.at[0])
    drain(all_evals.at[pl.ds(0, 15)], evals_sem.at[0])
    drain(all_codes.at[pl.ds(0, 15)], codes_sem.at[0])
    drain(back_recv.at[pl.ds(0, 15)], back_sem.at[0])
    for _ in range(5):
        drain(precond.at[0, :, pl.ds(0, 3 * BLOCK)], precond_sem.at[0])
    drain(layer_recv.at[pl.ds(0, 31)], layer_sem.at[0])
    drain(final.at[pl.ds(0, 15)], final_sem.at[0])

    @pl.when(layer != chip)
    def _():
        drain(tile, final_sem.at[2])


def on_device(query_pool, query_ids, eigenbasis, eigenvalues, train_grads, train_ids):
    return pl.pallas_call(
        kernel,
        out_shape=jax.ShapeDtypeStruct((QUERIES, ROWS), F32),
        in_specs=[pl.BlockSpec(memory_space=pl.ANY)] * 6,
        out_specs=pl.BlockSpec(memory_space=pltpu.VMEM),
        scratch_shapes=[
            pltpu.VMEM((256, BLOCK), BF16),
            pltpu.VMEM((1, QUERIES), jnp.int32),
            pltpu.VMEM((1, BLOCK), F32),
            pltpu.VMEM((CORES, 1, ROWS), jnp.int32),
            pltpu.VMEM((CHIPS, BLOCK, CORES * BLOCK), BF16),
            pltpu.VMEM((SIDE, CORES * ROWS, SIDE * BLOCK), BF16),
            pltpu.VMEM((SIDE, CORES * ROWS, SIDE * BLOCK), BF16),
            pltpu.VMEM((SIDE, QUERIES, SIDE * BLOCK), BF16),
            pltpu.VMEM((QUERIES, BLOCK), BF16),
            pltpu.VMEM((CHIPS, 1, BLOCK), F32),
            pltpu.VMEM((2, 8, CORES * BLOCK), F32),
            pltpu.VMEM((QUERIES, CORES * BLOCK), F32),
            pltpu.VMEM((QUERIES, CORES * BLOCK), F32),
            pltpu.VMEM((CORES, 1, ROWS), jnp.int32),
            pltpu.VMEM((CHIPS, CORES, 1, ROWS), jnp.int32),
            pltpu.VMEM((SIDE, QUERIES, SIDE * BLOCK), BF16),
            pltpu.VMEM((CHIPS, QUERIES, BLOCK), BF16),
            pltpu.VMEM((QUERIES, BLOCK), BF16),
            pltpu.VMEM((SIDE, QUERIES, SIDE * BLOCK), BF16),
            pltpu.VMEM((ROWS, BLOCK), F32),
            pltpu.VMEM((CORES * LAYERS, 8, BLOCK), F32),
            pltpu.VMEM((8, BLOCK), F32),
            pltpu.VMEM((CHIPS, 8, BLOCK), F32),
            pltpu.SemaphoreType.DMA((5,)),
            pltpu.SemaphoreType.DMA((2,)),
            pltpu.SemaphoreType.DMA((3,)),
            pltpu.SemaphoreType.DMA((2,)),
            pltpu.SemaphoreType.DMA((1 + len(PARTS) * SIDE,)),
            pltpu.SemaphoreType.DMA((4,)),
            pltpu.SemaphoreType.DMA((1 + len(PARTS),)),
            pltpu.SemaphoreType.DMA((2,)),
            pltpu.SemaphoreType.DMA((1 + len(PARTS) * SIDE,)),
            pltpu.SemaphoreType.DMA((1 + len(PARTS) * SIDE,)),
            pltpu.SemaphoreType.DMA((2,)),
            pltpu.SemaphoreType.DMA((3,)),
        ],
        compiler_params=pltpu.CompilerParams(
            collective_id=0, has_side_effects=True, vmem_limit_bytes=40 * 1024 * 1024
        ),
        cost_estimate=pl.CostEstimate(flops=600_000_000, bytes_accessed=4_000_000, transcendentals=0),
    )(
        *[
            pltpu.with_memory_space_constraint(array, pltpu.HBM)
            for array in (
                query_pool,
                query_ids.reshape(1, QUERIES),
                eigenbasis.reshape(1, CHIPS, CORES, BLOCK, BLOCK),
                eigenvalues,
                train_grads,
                train_ids.reshape(1, ROWS),
            )
        ]
    )


def solution(mesh):
    in_specs = (
        P("layer", None, "blk"),
        P(),
        P("layer", None, "blk"),
        P("layer", "blk"),
        P("layer", "blk", None),
        P("blk"),
    )
    out_specs = P(None, "blk")
    return jax.shard_map(
        on_device, mesh=mesh, in_specs=in_specs, out_specs=out_specs, check_vma=False
    )
```

```python
import jax
import jax.numpy as jnp
from jax import lax
from jax.experimental import pallas as pl
from jax.experimental.pallas import tpu as pltpu
from jax.sharding import PartitionSpec as P

WIDTH = 4096
QUERIES = 64
PARTS = ((0, 32), (32, 32))
LAG = 0
LAYERS = 16
CHIPS = 16
CORES = 2
SIDE = 4
LAYER_STEPS = (8, 9, 7, 10, 6, 11, 5, 12, 4, 13, 3, 14, 2, 15, 1, 0)
BLOCK = 128
ROWS = 256
MESH = pl.DeviceIdType.MESH
F32 = jnp.float32
BF16 = jnp.bfloat16


def split3(value):
    first = value.astype(BF16)
    rest = value - first.astype(F32)
    second = rest.astype(BF16)
    third = (rest - second.astype(F32)).astype(BF16)
    return first, second, third


def dot(a, b, a_dim, b_dim):
    return lax.dot_general(a, b, (((a_dim,), (b_dim,)), ((), ())), preferred_element_type=F32)


def owner_order(ids):
    owner = ids // ROWS
    slot = ids - owner * ROWS
    member = (lax.broadcasted_iota(jnp.int32, (32, ROWS), 0) == owner).astype(F32)
    before = lax.broadcasted_iota(jnp.int32, (ROWS, ROWS), 0) < lax.broadcasted_iota(jnp.int32, (ROWS, ROWS), 1)
    counts = dot(member.astype(BF16), before.astype(F32).astype(BF16), 1, 0)
    rank = jnp.sum(member * counts, axis=0, keepdims=True)
    place = owner * 8 + rank.astype(jnp.int32)
    hit = lax.broadcasted_iota(jnp.int32, (ROWS, ROWS), 0) == place
    return hit.astype(F32).astype(BF16), place * ROWS + slot


def kernel(
    pool_hbm, qids_hbm, eigen_hbm, evals_hbm, train_hbm, tids_hbm, out_ref,
    pool, qids, evals, ids, basis, train, sorted_train, gathered, message, all_evals, pair_evals, pair_send, pair_recv,
    codes, all_codes, back_send, back_recv, piece, precond, scores, layer_recv, tile, final,
    local_sem, basis_sem, train_sem, ids_sem, gather_sem, evals_sem, pair_sem, codes_sem, back_sem, precond_sem,
    layer_sem, final_sem,
):
    layer = lax.axis_index("layer")
    blk = lax.axis_index("blk")
    chip = blk // CORES
    core = blk - chip * CORES
    z_hi = chip // SIDE
    x = chip - z_hi * SIDE
    twin = chip * CORES + (1 - core)

    others = [
        (2, 2), (1, 2), (3, 2), (2, 1), (2, 3), (1, 1), (3, 3), (2, 0), (1, 3), (3, 1), (1, 0), (3, 0), (0, 2), (0, 1), (0, 3)
    ]

    def peer(dz, dx):
        return lax.rem(z_hi + dz, SIDE) * SIDE + lax.rem(x + dx, SIDE)

    def remote(src, dst, send, recv, to_layer, to_blk):
        return pltpu.make_async_remote_copy(
            src_ref=src, dst_ref=dst, send_sem=send, recv_sem=recv,
            device_id=(to_layer, to_blk), device_id_type=MESH,
        )

    def drain(ref, sem):
        pltpu.make_async_copy(ref, ref, sem).wait()

    barrier = pltpu.get_barrier_semaphore()
    for dz, dx in others:
        pl.semaphore_signal(barrier, inc=1, device_id=(layer, peer(dz, dx) * CORES + core), device_id_type=MESH)
    pl.semaphore_signal(barrier, inc=1, device_id=(layer, twin), device_id_type=MESH)
    for step in range(1, LAYERS):
        other = lax.rem(layer + step, LAYERS)
        pl.semaphore_signal(barrier, inc=1, device_id=(other, blk), device_id_type=MESH)

    small = [
        pltpu.make_async_copy(pool_hbm.at[0], pool, local_sem.at[0]),
        pltpu.make_async_copy(qids_hbm, qids, local_sem.at[1]),
        pltpu.make_async_copy(evals_hbm, evals, local_sem.at[2]),
        pltpu.make_async_copy(tids_hbm, ids.at[core], local_sem.at[3]),
    ]
    for copy in small:
        copy.start()
    own_columns = pl.ds(pl.multiple_of(core * BLOCK, BLOCK), BLOCK)
    own_basis = pltpu.make_async_copy(eigen_hbm.at[0, :, core], basis.at[:, :, own_columns], local_sem.at[4])
    own_basis.start()
    own_rows = pl.ds(pl.multiple_of(core * ROWS, ROWS), ROWS)
    for copy in small:
        copy.wait()
    pick = (lax.broadcasted_iota(jnp.int32, (256, QUERIES), 0) == qids[...]).astype(F32).astype(BF16)
    message[...] = dot(pick, pool[...], 0, 0).astype(BF16)
    own_features = pl.ds(pl.multiple_of(x * BLOCK, BLOCK), BLOCK)
    gathered[z_hi, :, own_features] = message[...]
    all_evals[chip] = evals[...]

    pl.semaphore_wait(barrier, 15 + 1 + 15)

    for dz, dx in others:
        target = peer(dz, dx) * CORES + core
        remote(evals, all_evals.at[chip], evals_sem.at[0], evals_sem.at[1], layer, target).start()
    send_basis = remote(
        eigen_hbm.at[0, :, 1 - core], basis.at[:, :, own_columns], basis_sem.at[0], basis_sem.at[1], layer, twin
    )
    send_basis.start()
    for part, (first, count) in enumerate(PARTS):
        rows = pl.ds(first, count)
        for dz, dx in others:
            target = peer(dz, dx) * CORES + core
            remote(
                message.at[rows], gathered.at[z_hi, rows, own_features],
                gather_sem.at[0], gather_sem.at[1 + part * SIDE + dz], layer, target,
            ).start()
    send_ids = remote(ids.at[core], ids.at[core], ids_sem.at[0], ids_sem.at[1], layer, twin)
    send_ids.start()
    for index in range(CHIPS):
        kept = pl.ds(pl.multiple_of((index * CORES + core) * BLOCK, BLOCK), BLOCK)
        to_columns = pl.ds((index % SIDE) * BLOCK, BLOCK)
        pltpu.make_async_copy(
            train_hbm.at[0, :, kept], train.at[index // SIDE, own_rows, to_columns], train_sem.at[0]
        ).start()

    send_ids.wait()
    hit_0, codes_0 = owner_order(ids[0])
    hit_1, codes_1 = owner_order(ids[1])
    codes[0] = codes_0
    codes[1] = codes_1
    all_codes[chip, 0] = codes_0
    all_codes[chip, 1] = codes_1

    own_basis.wait()
    send_basis.wait()

    def row_of(dz):
        return lax.rem(z_hi + (SIDE - dz), SIDE)

    drain(all_evals.at[pl.ds(0, 15)], evals_sem.at[1])
    total = jnp.sum(all_evals[...][:, 0, :], keepdims=True)
    pair_lane = lax.broadcasted_iota(jnp.int32, (8, CORES * BLOCK), 1)
    pair_row = lax.broadcasted_iota(jnp.int32, (8, CORES * BLOCK), 0)
    mine = pair_lane // BLOCK == core
    wide = jnp.concatenate([evals[...], evals[...]], axis=1)
    pair_evals[0] = jnp.where(
        pair_row == 0, jnp.where(mine, wide, 0.0), jnp.where(pair_row == 1, total, 0.0)
    )
    send_evals = remote(pair_evals.at[0], pair_evals.at[1], evals_sem.at[2], evals_sem.at[3], layer, twin)
    send_evals.start()

    send_pair = []
    own_parts = []

    def rotate(part):
        first, count = PARTS[part]
        rotated = jnp.zeros((count, CORES * BLOCK), F32)
        for dz in (0, 1, 3, 2):
            row = row_of(dz)
            arrival = gather_sem.at[1 + part * SIDE + dz]
            if dz == 0:
                drain(gathered.at[0, pl.ds(0, count), pl.ds(0, 3 * BLOCK)], arrival)
            else:
                drain(gathered.at[0, pl.ds(0, count)], arrival)
            vectors = basis[pl.ds(row * SIDE, SIDE)].reshape(SIDE * BLOCK, CORES * BLOCK)
            rotated += dot(gathered[row, first : first + count, :], vectors, 1, 0)
        rows = pl.ds(first, count)
        pair_send[first : first + count, :] = rotated
        send_pair.append(
            remote(pair_send.at[rows], pair_recv.at[rows], pair_sem.at[0], pair_sem.at[1 + part], layer, twin)
        )
        send_pair[part].start()

    def send_back(part):
        first, count = PARTS[part]
        rows = pl.ds(first, count)
        send_pair[part].wait_recv()
        damped = ((pair_send[first : first + count, :] + pair_recv[first : first + count, :]) / divisor).astype(BF16)
        for dz in (2, 1, 3, 0):
            row = lax.rem(z_hi + dz, SIDE)
            vectors = basis[pl.ds(row * SIDE, SIDE)].reshape(SIDE * BLOCK, CORES * BLOCK)
            back_send[row, first : first + count, :] = dot(damped, vectors, 1, 1).astype(BF16)
            for dx in (2, 1, 3, 0):
                if dz == 0 and dx == 0:
                    continue
                column = lax.rem(x + dx, SIDE)
                block = pl.ds(pl.multiple_of(column * BLOCK, BLOCK), BLOCK)
                remote(
                    back_send.at[row, rows, block], back_recv.at[chip, rows],
                    back_sem.at[0], back_sem.at[1 + part * SIDE + dz], layer, (row * SIDE + column) * CORES + core,
                ).start()
        own_parts.append(dot(damped, basis[chip], 1, 1))
        back_recv[chip, first : first + count, :] = jnp.zeros((count, BLOCK), BF16)

    for part in range(len(PARTS) + LAG):
        if part < len(PARTS):
            rotate(part)
        if part == 0:
            send_evals.wait()
            both = pair_evals[0] + pair_evals[1]
            divisor = both[0:1, :] + 0.1 * both[1:2, :] / WIDTH
        if part >= LAG:
            send_back(part - LAG)

    for index in range(CHIPS):
        sent = pl.ds(pl.multiple_of((index * CORES + 1 - core) * BLOCK, BLOCK), BLOCK)
        to_columns = pl.ds((index % SIDE) * BLOCK, BLOCK)
        remote(
            train_hbm.at[0, :, sent], train.at[index // SIDE, own_rows, to_columns],
            train_sem.at[1], train_sem.at[2], layer, twin,
        ).start()

    for sem in range(3):
        drain(train.at[:, pl.ds(0, ROWS), :], train_sem.at[sem])
    for index in range(SIDE):
        sorted_train[index, 0:ROWS, :] = dot(hit_0, train[index, 0:ROWS, :], 1, 0).astype(BF16)
        sorted_train[index, ROWS : 2 * ROWS, :] = dot(hit_1, train[index, ROWS : 2 * ROWS, :], 1, 0).astype(BF16)

    for part, (first, count) in enumerate(PARTS):
        rows = pl.ds(first, count)
        precond_sum = own_parts[part]
        for dz in (0, 1, 3, 2):
            drain(back_recv.at[pl.ds(0, 3 if dz == 0 else 4), pl.ds(0, count)], back_sem.at[1 + part * SIDE + dz])
            arrived = back_recv[pl.ds(row_of(dz) * SIDE, SIDE), first : first + count, :]
            precond_sum += jnp.sum(arrived.astype(F32), axis=0)
        piece[first : first + count, :] = precond_sum.astype(BF16)
        precond[z_hi, first : first + count, own_features] = piece[first : first + count, :]
        for dz, dx in others:
            target = peer(dz, dx) * CORES + core
            remote(
                piece.at[rows], precond.at[z_hi, rows, own_features],
                precond_sem.at[0], precond_sem.at[1 + part * SIDE + dz], layer, target,
            ).start()

    by_query = jnp.zeros((QUERIES, CORES * ROWS), F32)
    for dz in (0, 1, 3, 2):
        row = row_of(dz)
        for part, (first, count) in enumerate(PARTS):
            arrival = precond_sem.at[1 + part * SIDE + dz]
            if dz == 0:
                drain(precond.at[0, pl.ds(0, count), pl.ds(0, 3 * BLOCK)], arrival)
            else:
                drain(precond.at[0, pl.ds(0, count)], arrival)
        by_query += dot(precond[row], sorted_train[row], 1, 1)
    by_core = jnp.concatenate([by_query[:, 0:ROWS], by_query[:, ROWS : 2 * ROWS]], axis=0)
    scores[...] = by_core.T
    mine_at = layer * CORES + core
    for step in LAYER_STEPS:
        other = lax.rem(layer + step, LAYERS)
        for flip in range(CORES):
            if step == 0 and flip == 0:
                continue
            to_core = core if flip == 0 else 1 - core
            rows = pl.ds(pl.multiple_of((other * CORES + to_core) * 8, 8), 8)
            remote(
                scores.at[rows, :], layer_recv.at[mine_at], layer_sem.at[0], layer_sem.at[1],
                other, chip * CORES + to_core,
            ).start()
    for dz, dx in others:
        target = peer(dz, dx) * CORES + core
        remote(codes, all_codes.at[chip], codes_sem.at[0], codes_sem.at[1], layer, target).start()
    layer_recv[mine_at] = scores[pl.ds(pl.multiple_of(mine_at * 8, 8), 8), :]

    drain(layer_recv.at[pl.ds(0, 31)], layer_sem.at[1])
    tile[...] = jnp.sum(layer_recv[...], axis=0)

    owner = layer * CORES + core
    for step in LAYER_STEPS:
        if step == 0:
            continue
        other = lax.rem(layer + step, LAYERS)
        remote(tile, final.at[chip], final_sem.at[0], final_sem.at[1], other, owner).start()

    @pl.when(layer != chip)
    def _():
        remote(tile, final.at[chip], final_sem.at[2], final_sem.at[1], layer, owner).start()

    @pl.when(layer == chip)
    def _():
        pltpu.make_async_copy(tile, final.at[chip], final_sem.at[1]).start()

    drain(all_codes.at[pl.ds(0, 15)], codes_sem.at[1])
    rank = lax.broadcasted_iota(jnp.int32, (CHIPS, 8, ROWS), 1)
    lane = lax.broadcasted_iota(jnp.int32, (CHIPS, 8, ROWS), 2).astype(F32)
    put = []
    for source in range(CORES):
        code = all_codes[:, source]
        place = code // ROWS
        slot = (code - place * ROWS).astype(F32)
        wanted = jnp.sum(jnp.where(place - 8 * blk == rank, slot, 0.0), axis=2, keepdims=True)
        put.append((wanted == lane).astype(F32).reshape(BLOCK, ROWS).astype(BF16))
    put = jnp.concatenate(put, axis=0)

    drain(final, final_sem.at[1])
    values = final[...].reshape(BLOCK, BLOCK).T
    values = jnp.concatenate([values[0:QUERIES, :], values[QUERIES : 2 * QUERIES, :]], axis=1)
    placed = dot(jnp.concatenate(split3(values), axis=0), put, 1, 0)
    placed = placed[0:QUERIES, :] + placed[QUERIES : 2 * QUERIES, :] + placed[2 * QUERIES : 3 * QUERIES, :]
    out_ref[...] = placed

    for _ in range(5):
        drain(gathered.at[0, :, pl.ds(0, 3 * BLOCK)], gather_sem.at[0])
    drain(pair_send, pair_sem.at[0])
    drain(all_evals.at[pl.ds(0, 15)], evals_sem.at[0])
    drain(all_codes.at[pl.ds(0, 15)], codes_sem.at[0])
    drain(back_recv.at[pl.ds(0, 15)], back_sem.at[0])
    for _ in range(5):
        drain(precond.at[0, :, pl.ds(0, 3 * BLOCK)], precond_sem.at[0])
    drain(layer_recv.at[pl.ds(0, 31)], layer_sem.at[0])
    drain(final.at[pl.ds(0, 15)], final_sem.at[0])

    @pl.when(layer != chip)
    def _():
        drain(tile, final_sem.at[2])


def on_device(query_pool, query_ids, eigenbasis, eigenvalues, train_grads, train_ids):
    return pl.pallas_call(
        kernel,
        out_shape=jax.ShapeDtypeStruct((QUERIES, ROWS), F32),
        in_specs=[pl.BlockSpec(memory_space=pl.ANY)] * 6,
        out_specs=pl.BlockSpec(memory_space=pltpu.VMEM),
        scratch_shapes=[
            pltpu.VMEM((256, BLOCK), BF16),
            pltpu.VMEM((1, QUERIES), jnp.int32),
            pltpu.VMEM((1, BLOCK), F32),
            pltpu.VMEM((CORES, 1, ROWS), jnp.int32),
            pltpu.VMEM((CHIPS, BLOCK, CORES * BLOCK), BF16),
            pltpu.VMEM((SIDE, CORES * ROWS, SIDE * BLOCK), BF16),
            pltpu.VMEM((SIDE, CORES * ROWS, SIDE * BLOCK), BF16),
            pltpu.VMEM((SIDE, QUERIES, SIDE * BLOCK), BF16),
            pltpu.VMEM((QUERIES, BLOCK), BF16),
            pltpu.VMEM((CHIPS, 1, BLOCK), F32),
            pltpu.VMEM((2, 8, CORES * BLOCK), F32),
            pltpu.VMEM((QUERIES, CORES * BLOCK), F32),
            pltpu.VMEM((QUERIES, CORES * BLOCK), F32),
            pltpu.VMEM((CORES, 1, ROWS), jnp.int32),
            pltpu.VMEM((CHIPS, CORES, 1, ROWS), jnp.int32),
            pltpu.VMEM((SIDE, QUERIES, SIDE * BLOCK), BF16),
            pltpu.VMEM((CHIPS, QUERIES, BLOCK), BF16),
            pltpu.VMEM((QUERIES, BLOCK), BF16),
            pltpu.VMEM((SIDE, QUERIES, SIDE * BLOCK), BF16),
            pltpu.VMEM((ROWS, BLOCK), F32),
            pltpu.VMEM((CORES * LAYERS, 8, BLOCK), F32),
            pltpu.VMEM((8, BLOCK), F32),
            pltpu.VMEM((CHIPS, 8, BLOCK), F32),
            pltpu.SemaphoreType.DMA((5,)),
            pltpu.SemaphoreType.DMA((2,)),
            pltpu.SemaphoreType.DMA((3,)),
            pltpu.SemaphoreType.DMA((2,)),
            pltpu.SemaphoreType.DMA((1 + len(PARTS) * SIDE,)),
            pltpu.SemaphoreType.DMA((4,)),
            pltpu.SemaphoreType.DMA((1 + len(PARTS),)),
            pltpu.SemaphoreType.DMA((2,)),
            pltpu.SemaphoreType.DMA((1 + len(PARTS) * SIDE,)),
            pltpu.SemaphoreType.DMA((1 + len(PARTS) * SIDE,)),
            pltpu.SemaphoreType.DMA((2,)),
            pltpu.SemaphoreType.DMA((3,)),
        ],
        compiler_params=pltpu.CompilerParams(
            collective_id=0, has_side_effects=True, vmem_limit_bytes=40 * 1024 * 1024
        ),
        cost_estimate=pl.CostEstimate(flops=600_000_000, bytes_accessed=4_000_000, transcendentals=0),
    )(
        *[
            pltpu.with_memory_space_constraint(array, pltpu.HBM)
            for array in (
                query_pool,
                query_ids.reshape(1, QUERIES),
                eigenbasis.reshape(1, CHIPS, CORES, BLOCK, BLOCK),
                eigenvalues,
                train_grads,
                train_ids.reshape(1, ROWS),
            )
        ]
    )


def solution(mesh):
    in_specs = (
        P("layer", None, "blk"),
        P(),
        P("layer", None, "blk"),
        P("layer", "blk"),
        P("layer", "blk", None),
        P("blk"),
    )
    out_specs = P(None, "blk")
    return jax.shard_map(
        on_device, mesh=mesh, in_specs=in_specs, out_specs=out_specs, check_vma=False
    )
```
